32 devices in a mesh: rows: 8 (over y, x, core), grp: 4 (over z).
Axes of the slice: x: 2, y: 2, z: 4, core: 2. Of those that a mesh axis runs over, the one named last changes fastest.
Arguments:
- embeddings: bfloat16 [65536, 1024], P('rows', 'grp'), may hold values from -6 to 6
- fine_local: int32 [65536], P('rows'), may hold values from 0 to 2047
- send_counts: int32 [8, 8], P('rows'), may hold values from 0 to 2048, as said below
- old_fine: bfloat16 [16384, 1024], P('rows', 'grp'), may hold values from -6 to 6
- coarse_ids: int32 [16384], P('rows'), may hold values from 0 to 2047, as said below
- old_coarse: bfloat16 [2048, 1024], P('rows', 'grp'), may hold values from -6 to 6
Outputs:
- new_fine: bfloat16 [16384, 1024], P('rows', 'grp')
- coarse_dirs: bfloat16 [2048, 1024], P('rows')
The draws below stay inside these ranges and needn't reach their ends.
Inputs may be any that keep to these rules, and one draw needn't show every extreme that they name: Row d of send_counts splits the 8192 rows of block d, in order, into segments for owners 0, 1, ...; each row of send_counts sums to 8192; one owner receives exactly 2048 rows from every block. `coarse_ids`: within each block of 2048 consecutive level-1 clusters, at most 512 have a level-2 cluster in any one block of 256 consecutive level-2 clusters; one such block reaches that from every block.
All inputs are finite; a program needn't handle non-finite values.
Results may differ from the reference program's by a relative error of at most 0.006.
Values may be sent and summed in bfloat16 or wider, within the bound.
A program may use at most 64 MiB of HBM per device.

```python
import jax
import jax.numpy as jnp
from jax import lax

D = 1024
R_DEV = 8192
K1_DEV = 2048
K2_DEV = 256
K1 = 16384
K2 = 2048
NROWS = 65536
N_ROWS = 8


def owner_loads(key, devices, total):
    mean_load = total // devices
    order = jax.random.permutation(jax.random.fold_in(key, 1), devices)
    half = devices // 2
    heavy = order[:half]
    light = order[half:]
    shift = jax.random.randint(jax.random.fold_in(key, 2), (devices, half), mean_load // 2, mean_load + 1)
    shift = shift.at[:, 0].set(mean_load)
    loads = jnp.full((devices, devices), mean_load, jnp.int32)
    loads = loads.at[:, heavy].add(shift).at[:, light].add(-shift)
    return loads.astype(jnp.int32)


def draw_send_counts(key, part):
    return owner_loads(jax.random.fold_in(key, 3), N_ROWS, R_DEV)


def draw_coarse_ids(key, part):
    loads = owner_loads(jax.random.fold_in(key, 7), N_ROWS, K1_DEV)
    ends = jnp.cumsum(loads, axis=1)
    position = jnp.arange(K1_DEV, dtype=jnp.int32)
    owners = jnp.sum((ends[:, None, :] <= position[None, :, None]).astype(jnp.int32), axis=2).astype(jnp.int32)
    shuffle_keys = jax.random.split(jax.random.fold_in(key, 8), N_ROWS)
    owners = jax.vmap(lambda k, o: jax.random.permutation(k, o))(shuffle_keys, owners)
    local_id = jax.random.randint(jax.random.fold_in(key, 9), (N_ROWS, K1_DEV), 0, K2_DEV)
    return (owners * K2_DEV + local_id).reshape(-1).astype(jnp.int32)


def place_ends(drawn, stream_key, least, top_value):
    extent = drawn.shape
    spot = [jax.random.randint(jax.random.fold_in(stream_key, axis), (), 0, extent[axis]) for axis in range(len(extent))]
    drawn = drawn.at[tuple(spot)].set(least)
    longest = extent.index(max(extent))
    spot[longest] = (spot[longest] + 1) % extent[longest]
    return drawn.at[tuple(spot)].set(top_value)


def shard_levels(key, shape, shards, least, top_value):
    def one(axis_at, blocks):
        heights = jax.random.uniform(jax.random.fold_in(jax.random.fold_in(key, 6), axis_at), (blocks,), jnp.float32, least / len(shards), top_value / len(shards))
        return jnp.repeat(jnp.exp(heights), shape[axis_at] // blocks).reshape((-1,) + (1,) * (len(shape) - axis_at - 1))

    factor_of = one(*shards[0])
    for cut in shards[1:]:
        factor_of = factor_of * one(*cut)
    return factor_of


def noise(rng, extent, deviation, reach, shards=(), kind=jnp.bfloat16):
    array = deviation * jax.random.normal(rng, extent, jnp.float32)
    if shards:
        array = array * shard_levels(rng, extent, shards, -0.22, 0.18)
    return jnp.clip(array, -reach, reach).astype(kind)


def setup_inputs(seed: int = 0) -> dict:
    seeds = jax.random.split(jax.random.key(seed), 7)
    embeddings = noise(seeds[0], (NROWS, D), 1.0, 6.0, ((0, 8), (1, 4)))
    fine_local = place_ends(jax.random.randint(seeds[1], (NROWS,), 0, K1_DEV), jax.random.fold_in(seeds[1], 1), 0, K1_DEV - 1).astype(jnp.int32)
    send_counts = draw_send_counts(jax.random.fold_in(seeds[6], 71), 0)
    old_fine = noise(seeds[3], (K1, D), 1.0, 6.0, ((0, 8), (1, 4)))
    coarse_ids = draw_coarse_ids(jax.random.fold_in(seeds[6], 71), 0)
    old_coarse = noise(seeds[5], (K2, D), 1.0, 6.0, ((0, 8), (1, 4)))
    return {"embeddings": embeddings, "fine_local": fine_local, "send_counts": send_counts, "old_fine": old_fine, "coarse_ids": coarse_ids, "old_coarse": old_coarse}


def segment_owner(send_counts, per_block):
    ends = jnp.cumsum(send_counts, axis=1)
    position = jnp.arange(per_block, dtype=jnp.int32)
    below = (ends[:, None, :] <= position[None, :, None]).astype(jnp.int32)
    return lax.optimization_barrier(jnp.sum(below, axis=2)).astype(jnp.int32)

def reference(embeddings, fine_local, send_counts, old_fine, coarse_ids, old_coarse):
    block_count = send_counts.shape[0]
    per_block = fine_local.shape[0] // block_count
    owners = segment_owner(send_counts, per_block).reshape(-1)
    fine_ids = (owners * K1_DEV + fine_local).astype(jnp.int32)
    fine_sums = jax.ops.segment_sum(embeddings.astype(jnp.float32), fine_ids, num_segments=K1)
    fine_counts = jax.ops.segment_sum(jnp.ones(fine_ids.shape, jnp.float32), fine_ids, num_segments=K1)
    new_fine = ((fine_sums + old_fine.astype(jnp.float32)) / (fine_counts + 1.0)[:, None]).astype(jnp.bfloat16)
    coarse_sums = jax.ops.segment_sum(new_fine.astype(jnp.float32), coarse_ids, num_segments=K2)
    coarse_counts = jax.ops.segment_sum(jnp.ones(coarse_ids.shape, jnp.float32), coarse_ids, num_segments=K2)
    coarse_means = (coarse_sums + old_coarse.astype(jnp.float32)) / (coarse_counts + 1.0)[:, None]
    scale = lax.rsqrt(lax.optimization_barrier(jnp.mean(coarse_means * coarse_means, axis=1, keepdims=True)) + 1e-06)
    coarse_dirs = (coarse_means * scale).astype(jnp.bfloat16)
    return (new_fine, coarse_dirs)
```

```python
import functools
import math

import jax
import jax.numpy as jnp
from jax import lax
from jax.experimental import pallas as pl
from jax.experimental.pallas import tpu as pltpu
from jax.sharding import PartitionSpec as P

MESH = pl.DeviceIdType.MESH
LANES = 128


def neighbours(me):
    core, x, y = me % 2, (me // 2) % 2, me // 4
    other_x, other_y = 1 - x, 1 - y
    partner = 1 - core + 2 * x + 4 * y
    along = {
        (0, 0): me,
        (1, 0): core + 2 * other_x + 4 * y,
        (0, 1): core + 2 * x + 4 * other_y,
        (1, 1): core + 2 * other_x + 4 * other_y,
    }
    return partner, along


def enter(targets):
    barrier = pltpu.get_barrier_semaphore()
    for target in targets:
        pl.semaphore_signal(barrier, inc=1, device_id={"rows": target}, device_id_type=MESH)
    pl.semaphore_wait(barrier, len(targets))


FIRST = ((1, 1, 0), (1, 1, 1), (1, 0, 0), (0, 1, 1), (1, 0, 1), (0, 1, 0))


def fine_kernel(
    tiles,
    emb,
    gid,
    first_tile,
    old,
    out,
    other_emb,
    other_gid,
    other_first,
    acc,
    hits,
    away,
    landed,
    counts,
    own_counts,
    landed_counts,
    swap_send,
    swap_recv,
    meta_sem,
    send_sem,
    recv_sem,
    count_send,
    count_recv,
):
    me = lax.axis_index("rows")
    partner, along = neighbours(me)
    fine_dev = old.shape[0]
    half = fine_dev // 2
    label_rows = gid.shape[0] - 8
    enter([partner, along[1, 0], along[0, 1], along[1, 1]])

    def remote(src, dst, send, recv, target):
        return pltpu.make_async_remote_copy(
            src_ref=src,
            dst_ref=dst,
            send_sem=send,
            recv_sem=recv,
            device_id={"rows": target},
            device_id_type=MESH,
        )

    swaps = [
        remote(gid, other_gid, swap_send.at[0], swap_recv.at[0], partner),
        remote(emb, other_emb, swap_send.at[1], swap_recv.at[1], partner),
    ]
    for copy in swaps:
        copy.start()
    swaps[0].wait_recv()
    meta = pltpu.make_async_copy(other_gid.at[pl.ds(label_rows, 8)], other_first, meta_sem)
    meta.start()
    meta.wait()
    swaps[1].wait_recv()

    counts[...] = jnp.zeros_like(counts)
    index = lax.broadcasted_iota(jnp.int32, (half, LANES), 0)

    def sums(owner, part, total):
        base = owner * fine_dev + part * half
        start_a = first_tile[0, owner]
        start_b = other_first[0, 0, owner]
        total[...] = jnp.zeros_like(total)
        hits[...] = jnp.zeros_like(hits)

        @pl.loop(0, tiles)
        def _(step):
            tile_a = start_a + step
            tile_b = start_b + step
            hot_a = jnp.where(index == gid[tile_a] - base, 1.0, 0.0).astype(jnp.bfloat16)
            hot_b = jnp.where(index == other_gid[tile_b] - base, 1.0, 0.0).astype(
                jnp.bfloat16
            )
            rows_a = emb[tile_a]
            rows_b = other_emb[tile_b]
            total[...] += jnp.dot(
                jnp.concatenate([hot_a, hot_b], axis=1),
                jnp.concatenate([rows_a, rows_b], axis=0),
                preferred_element_type=jnp.float32,
            )
            hits[...] += hot_a + hot_b

        return lax.dot_general(
            jnp.ones((8, LANES), jnp.bfloat16),
            hits[...],
            (((1,), (1,)), ((), ())),
            preferred_element_type=jnp.float32,
        )[0:1]

    sends = []
    for slot, (qx, qy, part) in enumerate(FIRST):
        counts[pl.ds(slot, 1), :] = sums(along[qx, qy], part, acc.at[0])
        if slot == 5:
            count_copies = []
            for place, (cx, cy) in enumerate(((1, 0), (0, 1), (1, 1))):
                copy = remote(
                    counts,
                    landed_counts.at[place],
                    count_send.at[place],
                    count_recv.at[place],
                    along[cx, cy],
                )
                copy.start()
                count_copies.append(copy)
        if slot >= 4:
            sends[5 - slot].wait_recv()
            away[slot] = (acc[0] + landed[5 - slot].astype(jnp.float32)).astype(jnp.bfloat16)
        else:
            away[slot] = acc[0].astype(jnp.bfloat16)
        target = along[1, 0] if slot % 2 == 0 else along[0, 1]
        copy = remote(away.at[slot], landed.at[slot], send_sem.at[slot], recv_sem.at[slot], target)
        copy.start()
        sends.append(copy)
    for part in range(2):
        own_counts[pl.ds(part, 1), :] = sums(me, part, acc.at[part])
    for copy in count_copies:
        copy.wait_recv()
    for part in range(2):
        seen = own_counts[pl.ds(part, 1), :]
        for place, quad in enumerate(((1, 0), (0, 1), (1, 1))):
            row = FIRST.index(quad + (part,))
            seen = seen + landed_counts[place, pl.ds(row, 1), :]
        divisor = jnp.broadcast_to(seen + 1.0, (LANES, half)).T
        divisor = jnp.concatenate([divisor] * (old.shape[1] // LANES), axis=1)
        near, far = (2, 5) if part == 0 else (3, 4)
        sends[near].wait_recv()
        sends[far].wait_recv()
        span = pl.ds(part * half, half)
        total = acc[part] + landed[near].astype(jnp.float32) + landed[far].astype(jnp.float32)
        out[span, :] = ((total + old[span, :].astype(jnp.float32)) / divisor).astype(jnp.bfloat16)
    for copy in swaps + sends + count_copies:
        copy.wait_send()


def fine_level(embeddings, fine_local, send_counts, old_fine):
    peers = lax.axis_size("rows")
    per_dev, width = embeddings.shape
    fine_dev = old_fine.shape[0]
    half = fine_dev // 2
    capacity = 2 * per_dev // peers
    tiles = capacity // LANES + 1
    position = jnp.arange(per_dev, dtype=jnp.int32)
    before = jnp.arange(peers)[None, :] < jnp.arange(peers)[:, None]
    starts = jnp.sum(jnp.where(before, send_counts, 0), axis=1)
    ends = starts + send_counts[0]
    owner = jnp.sum((ends[:, None] <= position[None, :]).astype(jnp.int32), axis=0)
    label_rows = per_dev // LANES
    first_tile = jnp.minimum(starts // LANES, label_rows - tiles)[None, :]
    gid = (owner * fine_dev + fine_local).reshape(label_rows, LANES)
    gid = jnp.concatenate([gid, jnp.pad(first_tile, ((0, 7), (0, LANES - peers)))], axis=0)
    gid = gid[:, None, :]
    tiled = embeddings.reshape(label_rows, LANES, width)
    vmem = pl.BlockSpec(memory_space=pltpu.VMEM)
    dma = pltpu.SemaphoreType.DMA
    return pl.pallas_call(
        functools.partial(fine_kernel, tiles),
        out_shape=jax.ShapeDtypeStruct(old_fine.shape, jnp.bfloat16),
        in_specs=[vmem, vmem, pl.BlockSpec(memory_space=pltpu.SMEM), vmem],
        out_specs=vmem,
        scratch_shapes=[
            pltpu.VMEM(tiled.shape, jnp.bfloat16),
            pltpu.VMEM(gid.shape, jnp.int32),
            pltpu.SMEM((8, 1, LANES), jnp.int32),
            pltpu.VMEM((2, half, width), jnp.float32),
            pltpu.VMEM((half, LANES), jnp.bfloat16),
            pltpu.VMEM((6, half, width), jnp.bfloat16),
            pltpu.VMEM((6, half, width), jnp.bfloat16),
            pltpu.VMEM((8, half), jnp.float32),
            pltpu.VMEM((8, half), jnp.float32),
            pltpu.VMEM((3, 8, half), jnp.float32),
            dma((2,)),
            dma((2,)),
            dma,
            dma((6,)),
            dma((6,)),
            dma((3,)),
            dma((3,)),
        ],
        compiler_params=pltpu.CompilerParams(
            collective_id=0, has_side_effects=True, vmem_limit_bytes=48 * 1024 * 1024
        ),
    )(tiled, gid, first_tile, old_fine)


def onehot_sums(arrived, arrived_labels, fine_dev):
    slot_total = arrived.shape[0]
    width = arrived.shape[1]
    block_rows = math.gcd(slot_total, 2048)
    block_count = slot_total // block_rows
    cluster_index = jnp.arange(fine_dev, dtype=jnp.int32)

    def accumulate(state_pair, pieces):
        fine_sums, totals = state_pair
        row_block, label_block = pieces
        onehot = cluster_index[:, None] == label_block[None, :]
        fine_sums = fine_sums + jnp.dot(
            onehot.astype(jnp.bfloat16), row_block, preferred_element_type=jnp.float32
        )
        totals = totals + jnp.sum(onehot.astype(jnp.int32), axis=1)
        return ((fine_sums, totals), None)

    start_state = (jnp.zeros((fine_dev, width), jnp.float32), jnp.zeros((fine_dev,), jnp.int32))
    (fine_sums, totals), _ = lax.scan(
        accumulate,
        start_state,
        (
            arrived.reshape(block_count, block_rows, width),
            arrived_labels.reshape(block_count, block_rows),
        ),
    )
    return (fine_sums, totals.astype(jnp.float32))


def exchanged_rows(embeddings, fine_local, send_counts, old_fine):
    peer_count = lax.axis_size("rows")
    per_dev = embeddings.shape[0]
    quarter = embeddings.shape[1]
    fine_dev = old_fine.shape[0]
    capacity = 2 * per_dev // peer_count
    counts = send_counts[0]
    starts = jnp.cumsum(counts) - counts
    offset = jnp.arange(capacity, dtype=jnp.int32)
    is_live = offset[None, :] < counts[:, None]
    padded_rows = jnp.concatenate(
        [embeddings, jnp.zeros((capacity, quarter), jnp.bfloat16)], axis=0
    )
    padded_local = jnp.concatenate([fine_local, jnp.zeros((capacity,), jnp.int32)], axis=0)

    def take_segment(first_row):
        segment_rows = lax.dynamic_slice_in_dim(padded_rows, first_row, capacity, 0)
        segment_labels = lax.dynamic_slice_in_dim(padded_local, first_row, capacity, 0)
        return (segment_rows, segment_labels)

    outgoing, raw_labels = lax.map(take_segment, starts)
    outgoing = jnp.where(is_live[:, :, None], outgoing, jnp.zeros((), jnp.bfloat16))
    labels = jnp.where(is_live, raw_labels, -1)
    arrived, arrived_labels = (
        lax.all_to_all(outgoing, "rows", split_axis=0, concat_axis=0, tiled=True),
        lax.all_to_all(labels, "rows", split_axis=0, concat_axis=0, tiled=True),
    )
    fine_sums, totals = onehot_sums(
        arrived.reshape(-1, quarter), arrived_labels.reshape(-1), fine_dev
    )
    new_fine = ((fine_sums + old_fine.astype(jnp.float32)) / (totals + 1.0)[:, None]).astype(
        jnp.bfloat16
    )
    return new_fine


def on_device(embeddings, fine_local, send_counts, old_fine, coarse_ids, old_coarse):
    peer_count = lax.axis_size("rows")
    quarter = embeddings.shape[1]
    fine_dev = old_fine.shape[0]
    coarse_dev = old_coarse.shape[0]
    tree = peer_count == 8 and 2 * embeddings.shape[0] // peer_count >= fine_dev
    level = fine_level if tree else exchanged_rows
    new_fine = level(embeddings, fine_local, send_counts, old_fine)
    owners = coarse_ids // coarse_dev
    local_id = coarse_ids - owners * coarse_dev
    capacity_two = 2 * fine_dev // peer_count
    member = (owners[:, None] == jnp.arange(peer_count, dtype=jnp.int32)[None, :]).astype(jnp.int32)
    slot_rank = jnp.sum(jnp.cumsum(member, axis=0) * member, axis=1) - 1
    slot_pos = owners * capacity_two + slot_rank
    placement = (
        jnp.arange(peer_count * capacity_two, dtype=jnp.int32)[:, None] == slot_pos[None, :]
    ).astype(jnp.bfloat16)
    outgoing_two = jnp.dot(placement, new_fine, preferred_element_type=jnp.float32).astype(
        jnp.bfloat16
    )
    label_plus = jnp.dot(
        placement, (local_id + 1).astype(jnp.bfloat16), preferred_element_type=jnp.float32
    )
    labels_two = label_plus.astype(jnp.int32) - 1
    received, received_labels = (
        lax.all_to_all(
            outgoing_two.reshape(peer_count, capacity_two, quarter),
            "rows",
            split_axis=0,
            concat_axis=0,
            tiled=True,
        ),
        lax.all_to_all(
            labels_two.reshape(peer_count, capacity_two),
            "rows",
            split_axis=0,
            concat_axis=0,
            tiled=True,
        ),
    )
    onehot_two = (
        jnp.arange(coarse_dev, dtype=jnp.int32)[:, None] == received_labels.reshape(-1)[None, :]
    )
    coarse_sums = jnp.dot(
        onehot_two.astype(jnp.bfloat16),
        received.reshape(-1, quarter),
        preferred_element_type=jnp.float32,
    )
    coarse_totals = jnp.sum(onehot_two.astype(jnp.int32), axis=1).astype(jnp.float32)
    coarse_means = (coarse_sums + old_coarse.astype(jnp.float32)) / (coarse_totals + 1.0)[:, None]
    squares = lax.psum(jnp.sum(coarse_means * coarse_means, axis=1), "grp")
    total_width = quarter * lax.axis_size("grp")
    unit_part = (coarse_means * lax.rsqrt(squares / total_width + 1e-06)[:, None]).astype(
        jnp.bfloat16
    )
    coarse_dirs = lax.all_gather(unit_part, "grp", axis=1, tiled=True)
    return (new_fine, coarse_dirs)


def solution(mesh):
    in_specs = (
        P("rows", "grp"),
        P("rows"),
        P("rows", None),
        P("rows", "grp"),
        P("rows"),
        P("rows", "grp"),
    )
    out_specs = (P("rows", "grp"), P("rows", None))
    return jax.shard_map(
        on_device, mesh=mesh, in_specs=in_specs, out_specs=out_specs, check_vma=False
    )
```

```python
import functools
import math

import jax
import jax.numpy as jnp
from jax import lax
from jax.experimental import pallas as pl
from jax.experimental.pallas import tpu as pltpu
from jax.sharding import PartitionSpec as P

MESH = pl.DeviceIdType.MESH
LANES = 128


def neighbours(me):
    core, x, y = me % 2, (me // 2) % 2, me // 4
    other_x, other_y = 1 - x, 1 - y
    partner = 1 - core + 2 * x + 4 * y
    along = {
        (0, 0): me,
        (1, 0): core + 2 * other_x + 4 * y,
        (0, 1): core + 2 * x + 4 * other_y,
        (1, 1): core + 2 * other_x + 4 * other_y,
    }
    return partner, along


FIRST = ((1, 1, 0), (1, 1, 1), (1, 0, 0), (0, 1, 1), (1, 0, 1), (0, 1, 0))
AWAY = ((1, 1), (1, 0), (0, 1))
META = 8


def one_hot(index, ids):
    low = jnp.clip(ids, -1, index.shape[0]).astype(jnp.int16)
    same = index == jnp.broadcast_to(low, index.shape)
    return jnp.where(same, jnp.ones((), jnp.bfloat16), jnp.zeros((), jnp.bfloat16))


def levels_kernel(
    tiles,
    emb,
    ids,
    first_tile,
    old,
    old_coarse,
    out,
    dirs,
    other_emb,
    other_ids,
    other_first,
    acc,
    hits,
    away,
    landed,
    counts,
    own_counts,
    landed_counts,
    other_fine,
    coarse_away,
    coarse_landed,
    coarse_counts,
    coarse_counts_landed,
    means,
    squares,
    swap_send,
    swap_recv,
    meta_sem,
    send_sem,
    recv_sem,
    count_send,
    count_recv,
    fine_send,
    fine_recv,
    coarse_send,
    coarse_recv,
    coarse_count_send,
    coarse_count_recv,
    means_send,
    means_recv,
    squares_send,
    squares_recv,
):
    me = lax.axis_index("rows")
    slab = lax.axis_index("grp")
    slabs = lax.axis_size("grp")
    partner, along = neighbours(me)
    fine_dev, width = old.shape
    half = fine_dev // 2
    coarse_dev = old_coarse.shape[0]
    label_rows = emb.shape[0]
    fine_tiles = out.shape[0]
    others = [(slab + step) % slabs for step in range(1, slabs)]

    barrier = pltpu.get_barrier_semaphore()
    mates = [partner] + [along[quad] for quad in AWAY]
    for mate in mates:
        pl.semaphore_signal(barrier, inc=1, device_id={"rows": mate}, device_id_type=MESH)
    for other in others:
        pl.semaphore_signal(barrier, inc=1, device_id={"grp": other}, device_id_type=MESH)
    pl.semaphore_wait(barrier, len(mates) + len(others))

    def remote(src, dst, send, recv, target, axis="rows"):
        return pltpu.make_async_remote_copy(
            src_ref=src,
            dst_ref=dst,
            send_sem=send,
            recv_sem=recv,
            device_id={axis: target},
            device_id_type=MESH,
        )

    swaps = [
        remote(ids, other_ids, swap_send.at[0], swap_recv.at[0], partner),
        remote(emb, other_emb, swap_send.at[1], swap_recv.at[1], partner),
    ]
    for copy in swaps:
        copy.start()
    counts[...] = jnp.zeros_like(counts)
    coarse_counts[...] = jnp.zeros_like(coarse_counts)
    swaps[0].wait_recv()
    meta = pltpu.make_async_copy(other_ids.at[pl.ds(label_rows, META)], other_first, meta_sem)
    meta.start()
    meta.wait()
    swaps[1].wait_recv()

    index = lax.broadcasted_iota(jnp.int32, (half, LANES), 0).astype(jnp.int16)

    def add_tiles(total, rows_of, ids_of, steps, depth):
        def piece(tile):
            hots, rows = [], []
            for side in range(2):
                hots.append(one_hot(index, ids_of(side, tile)))
                rows.append(rows_of(side, tile))
            hits[...] += hots[0] + hots[1]
            return hots, rows

        @pl.loop(0, steps)
        def _(step):
            hots, rows = [], []
            for part in range(depth):
                more_hots, more_rows = piece(step * depth + part)
                hots += more_hots
                rows += more_rows
            total[...] += jnp.dot(
                jnp.concatenate(hots, axis=1),
                jnp.concatenate(rows, axis=0),
                preferred_element_type=jnp.float32,
            )

    def hit_row():
        return lax.dot_general(
            jnp.ones((8, LANES), jnp.bfloat16),
            hits[...],
            (((1,), (1,)), ((), ())),
            preferred_element_type=jnp.float32,
        )[0:1]

    def sums(owner, part, total):
        base = owner * fine_dev + part * half
        start = (first_tile[0, owner], other_first[0, 0, owner])
        total[...] = jnp.zeros_like(total)
        hits[...] = jnp.zeros_like(hits)

        def rows_of(side, tile):
            return (emb, other_emb)[side][start[side] + tile]

        def ids_of(side, tile):
            return (ids, other_ids)[side][start[side] + tile] - base

        add_tiles(total, rows_of, ids_of, tiles // DEPTH, DEPTH)
        return hit_row()

    sends = []
    for slot, (qx, qy, part) in enumerate(FIRST):
        counts[pl.ds(slot, 1), :] = sums(along[qx, qy], part, acc.at[0])
        if slot == 5:
            count_copies = []
            for place, quad in enumerate(AWAY):
                copy = remote(
                    counts,
                    landed_counts.at[place],
                    count_send.at[place],
                    count_recv.at[place],
                    along[quad],
                )
                copy.start()
                count_copies.append(copy)
        if slot >= 4:
            sends[5 - slot].wait_recv()
            away[slot] = (acc[0] + landed[5 - slot].astype(jnp.float32)).astype(jnp.bfloat16)
        else:
            away[slot] = acc[0].astype(jnp.bfloat16)
        target = along[1, 0] if slot % 2 == 0 else along[0, 1]
        copy = remote(away.at[slot], landed.at[slot], send_sem.at[slot], recv_sem.at[slot], target)
        copy.start()
        sends.append(copy)
    for part in range(2):
        own_counts[pl.ds(part, 1), :] = sums(me, part, acc.at[part])
    for copy in count_copies:
        copy.wait_recv()

    def column(row):
        return jnp.broadcast_to(row, (LANES, row.shape[1])).T

    fine_swaps = []
    for part in range(2):
        seen = own_counts[pl.ds(part, 1), :]
        for place, quad in enumerate(AWAY):
            row = FIRST.index(quad + (part,))
            seen = seen + landed_counts[place, pl.ds(row, 1), :]
        divisor = jnp.concatenate([column(seen + 1.0)] * (width // LANES), axis=1)
        near, far = (2, 5) if part == 0 else (3, 4)
        sends[near].wait_recv()
        sends[far].wait_recv()
        total = acc[part] + landed[near].astype(jnp.float32) + landed[far].astype(jnp.float32)
        total = total + old[pl.ds(part * half, half), :].astype(jnp.float32)
        span = pl.ds(part * (fine_tiles // 2), fine_tiles // 2)
        out[span] = (total / divisor).astype(jnp.bfloat16).reshape(-1, LANES, width)
        copy = remote(
            out.at[span], other_fine.at[span], fine_send.at[part], fine_recv.at[part], partner
        )
        copy.start()
        fine_swaps.append(copy)

    quads = AWAY + ((0, 0),)
    acc[0] = jnp.zeros_like(acc[0])
    hits[...] = jnp.zeros_like(hits)
    for copy in fine_swaps:
        copy.wait_recv()

    def place_of(coarse):
        owner = coarse // coarse_dev
        row = jnp.full_like(coarse, -1)
        for order, quad in enumerate(quads):
            inside = coarse - along[quad] * coarse_dev
            row = jnp.where(owner == along[quad], inside + order * coarse_dev, row)
        return row

    def fine_rows(side, tile):
        return (out, other_fine)[side][tile]

    def coarse_places(side, tile):
        return place_of((ids, other_ids)[side][label_rows + META + tile])

    add_tiles(acc.at[0], fine_rows, coarse_places, fine_tiles // DEPTH, DEPTH)
    coarse_counts[pl.ds(0, 1), :] = hit_row()
    coarse_copies = []
    for order, quad in enumerate(AWAY):
        coarse_away[order] = acc[0, pl.ds(order * coarse_dev, coarse_dev), :].astype(jnp.bfloat16)
        for copy in (
            remote(
                coarse_counts,
                coarse_counts_landed.at[order],
                coarse_count_send.at[order],
                coarse_count_recv.at[order],
                along[quad],
            ),
            remote(
                coarse_away.at[order],
                coarse_landed.at[order],
                coarse_send.at[order],
                coarse_recv.at[order],
                along[quad],
            ),
        ):
            copy.start()
            coarse_copies.append(copy)
    total = acc[0, pl.ds(3 * coarse_dev, coarse_dev), :] + old_coarse[...].astype(jnp.float32)
    seen = coarse_counts[pl.ds(0, 1), pl.ds(3 * coarse_dev, coarse_dev)]
    for copy in coarse_copies:
        copy.wait_recv()
    for order in range(3):
        total = total + coarse_landed[order].astype(jnp.float32)
        seen = seen + coarse_counts_landed[order, pl.ds(0, 1), pl.ds(order * coarse_dev, coarse_dev)]
    mean = total / jnp.concatenate([column(seen + 1.0)] * (width // LANES), axis=1)
    means[slab] = mean.astype(jnp.bfloat16)
    square = jnp.sum(mean * mean, axis=1, keepdims=True)
    squares[slab] = jnp.broadcast_to(square, (coarse_dev, LANES)).T[0:8]
    mean_copies = []
    for order, other in enumerate(others):
        for copy in (
            remote(
                squares.at[slab],
                squares.at[slab],
                squares_send.at[order],
                squares_recv.at[order],
                other,
                "grp",
            ),
            remote(
                means.at[slab],
                means.at[slab],
                means_send.at[order],
                means_recv.at[order],
                other,
                "grp",
            ),
        ):
            copy.start()
            mean_copies.append(copy)
    for copy in mean_copies:
        copy.wait_recv()
    square = squares[0, 0:1]
    for at in range(1, slabs):
        square = square + squares[at, 0:1]
    scale = column(lax.rsqrt(square / (width * slabs) + 1e-06))
    scale = jnp.concatenate([scale] * (width // LANES), axis=1)
    for at in range(slabs):
        dirs[:, at * width : (at + 1) * width] = (means[at].astype(jnp.float32) * scale).astype(
            jnp.bfloat16
        )
    for copy in swaps + sends + count_copies + fine_swaps + coarse_copies + mean_copies:
        copy.wait_send()


DEPTH = 2


def tree_levels(embeddings, fine_local, send_counts, old_fine, coarse_ids, old_coarse):
    peers = lax.axis_size("rows")
    slabs = lax.axis_size("grp")
    per_dev, width = embeddings.shape
    fine_dev = old_fine.shape[0]
    coarse_dev = old_coarse.shape[0]
    half = fine_dev // 2
    capacity = 2 * per_dev // peers
    tiles = -(-(capacity // LANES + 1) // DEPTH) * DEPTH
    position = jnp.arange(per_dev, dtype=jnp.int32)
    before = jnp.arange(peers)[None, :] < jnp.arange(peers)[:, None]
    starts = jnp.sum(jnp.where(before, send_counts, 0), axis=1)
    ends = starts + send_counts[0]
    owner = jnp.sum((ends[:, None] <= position[None, :]).astype(jnp.int32), axis=0)
    label_rows = per_dev // LANES
    fine_tiles = fine_dev // LANES
    first_tile = jnp.minimum(starts // LANES, label_rows - tiles)[None, :]
    ids = jnp.concatenate(
        [
            (owner * fine_dev + fine_local).reshape(label_rows, LANES),
            jnp.pad(first_tile, ((0, META - 1), (0, LANES - peers))),
            coarse_ids.reshape(fine_tiles, LANES),
        ],
        axis=0,
    )[:, None, :]
    tiled = embeddings.reshape(label_rows, LANES, width)
    vmem = pl.BlockSpec(memory_space=pltpu.VMEM)
    dma = pltpu.SemaphoreType.DMA
    f32, bf16 = jnp.float32, jnp.bfloat16
    new_fine, dirs = pl.pallas_call(
        functools.partial(levels_kernel, tiles),
        out_shape=[
            jax.ShapeDtypeStruct((fine_tiles, LANES, width), bf16),
            jax.ShapeDtypeStruct((coarse_dev, slabs * width), bf16),
        ],
        in_specs=[vmem, vmem, pl.BlockSpec(memory_space=pltpu.SMEM), vmem, vmem],
        out_specs=[vmem, vmem],
        scratch_shapes=[
            pltpu.VMEM(tiled.shape, bf16),
            pltpu.VMEM(ids.shape, jnp.int32),
            pltpu.SMEM((META, 1, LANES), jnp.int32),
            pltpu.VMEM((2, half, width), f32),
            pltpu.VMEM((half, LANES), bf16),
            pltpu.VMEM((6, half, width), bf16),
            pltpu.VMEM((6, half, width), bf16),
            pltpu.VMEM((8, half), f32),
            pltpu.VMEM((8, half), f32),
            pltpu.VMEM((3, 8, half), f32),
            pltpu.VMEM((fine_tiles, LANES, width), bf16),
            pltpu.VMEM((3, coarse_dev, width), bf16),
            pltpu.VMEM((3, coarse_dev, width), bf16),
            pltpu.VMEM((8, half), f32),
            pltpu.VMEM((3, 8, half), f32),
            pltpu.VMEM((slabs, coarse_dev, width), bf16),
            pltpu.VMEM((slabs, 8, coarse_dev), f32),
            dma((2,)),
            dma((2,)),
            dma,
            dma((6,)),
            dma((6,)),
            dma((3,)),
            dma((3,)),
            dma((2,)),
            dma((2,)),
            dma((3,)),
            dma((3,)),
            dma((3,)),
            dma((3,)),
            dma((slabs - 1,)),
            dma((slabs - 1,)),
            dma((slabs - 1,)),
            dma((slabs - 1,)),
        ],
        compiler_params=pltpu.CompilerParams(
            collective_id=0, has_side_effects=True, vmem_limit_bytes=48 * 1024 * 1024
        ),
    )(tiled, ids, first_tile, old_fine, old_coarse)
    return new_fine.reshape(old_fine.shape), dirs


def onehot_sums(arrived, arrived_labels, fine_dev):
    slot_total = arrived.shape[0]
    width = arrived.shape[1]
    block_rows = math.gcd(slot_total, 2048)
    block_count = slot_total // block_rows
    cluster_index = jnp.arange(fine_dev, dtype=jnp.int32)

    def accumulate(state_pair, pieces):
        fine_sums, totals = state_pair
        row_block, label_block = pieces
        onehot = cluster_index[:, None] == label_block[None, :]
        fine_sums = fine_sums + jnp.dot(
            onehot.astype(jnp.bfloat16), row_block, preferred_element_type=jnp.float32
        )
        totals = totals + jnp.sum(onehot.astype(jnp.int32), axis=1)
        return ((fine_sums, totals), None)

    start_state = (jnp.zeros((fine_dev, width), jnp.float32), jnp.zeros((fine_dev,), jnp.int32))
    (fine_sums, totals), _ = lax.scan(
        accumulate,
        start_state,
        (
            arrived.reshape(block_count, block_rows, width),
            arrived_labels.reshape(block_count, block_rows),
        ),
    )
    return (fine_sums, totals.astype(jnp.float32))


def exchanged_rows(embeddings, fine_local, send_counts, old_fine):
    peer_count = lax.axis_size("rows")
    per_dev = embeddings.shape[0]
    quarter = embeddings.shape[1]
    fine_dev = old_fine.shape[0]
    capacity = 2 * per_dev // peer_count
    counts = send_counts[0]
    starts = jnp.cumsum(counts) - counts
    offset = jnp.arange(capacity, dtype=jnp.int32)
    is_live = offset[None, :] < counts[:, None]
    padded_rows = jnp.concatenate(
        [embeddings, jnp.zeros((capacity, quarter), jnp.bfloat16)], axis=0
    )
    padded_local = jnp.concatenate([fine_local, jnp.zeros((capacity,), jnp.int32)], axis=0)

    def take_segment(first_row):
        segment_rows = lax.dynamic_slice_in_dim(padded_rows, first_row, capacity, 0)
        segment_labels = lax.dynamic_slice_in_dim(padded_local, first_row, capacity, 0)
        return (segment_rows, segment_labels)

    outgoing, raw_labels = lax.map(take_segment, starts)
    outgoing = jnp.where(is_live[:, :, None], outgoing, jnp.zeros((), jnp.bfloat16))
    labels = jnp.where(is_live, raw_labels, -1)
    arrived, arrived_labels = (
        lax.all_to_all(outgoing, "rows", split_axis=0, concat_axis=0, tiled=True),
        lax.all_to_all(labels, "rows", split_axis=0, concat_axis=0, tiled=True),
    )
    fine_sums, totals = onehot_sums(
        arrived.reshape(-1, quarter), arrived_labels.reshape(-1), fine_dev
    )
    new_fine = ((fine_sums + old_fine.astype(jnp.float32)) / (totals + 1.0)[:, None]).astype(
        jnp.bfloat16
    )
    return new_fine


def on_device(embeddings, fine_local, send_counts, old_fine, coarse_ids, old_coarse):
    peer_count = lax.axis_size("rows")
    quarter = embeddings.shape[1]
    fine_dev = old_fine.shape[0]
    coarse_dev = old_coarse.shape[0]
    dense = 2 * embeddings.shape[0] // peer_count >= fine_dev
    if peer_count == 8 and dense and 8 * coarse_dev == fine_dev:
        return tree_levels(embeddings, fine_local, send_counts, old_fine, coarse_ids, old_coarse)
    new_fine = exchanged_rows(embeddings, fine_local, send_counts, old_fine)
    owners = coarse_ids // coarse_dev
    local_id = coarse_ids - owners * coarse_dev
    capacity_two = 2 * fine_dev // peer_count
    member = (owners[:, None] == jnp.arange(peer_count, dtype=jnp.int32)[None, :]).astype(jnp.int32)
    slot_rank = jnp.sum(jnp.cumsum(member, axis=0) * member, axis=1) - 1
    slot_pos = owners * capacity_two + slot_rank
    placement = (
        jnp.arange(peer_count * capacity_two, dtype=jnp.int32)[:, None] == slot_pos[None, :]
    ).astype(jnp.bfloat16)
    outgoing_two = jnp.dot(placement, new_fine, preferred_element_type=jnp.float32).astype(
        jnp.bfloat16
    )
    label_plus = jnp.dot(
        placement, (local_id + 1).astype(jnp.bfloat16), preferred_element_type=jnp.float32
    )
    labels_two = label_plus.astype(jnp.int32) - 1
    received, received_labels = (
        lax.all_to_all(
            outgoing_two.reshape(peer_count, capacity_two, quarter),
            "rows",
            split_axis=0,
            concat_axis=0,
            tiled=True,
        ),
        lax.all_to_all(
            labels_two.reshape(peer_count, capacity_two),
            "rows",
            split_axis=0,
            concat_axis=0,
            tiled=True,
        ),
    )
    onehot_two = (
        jnp.arange(coarse_dev, dtype=jnp.int32)[:, None] == received_labels.reshape(-1)[None, :]
    )
    coarse_sums = jnp.dot(
        onehot_two.astype(jnp.bfloat16),
        received.reshape(-1, quarter),
        preferred_element_type=jnp.float32,
    )
    coarse_totals = jnp.sum(onehot_two.astype(jnp.int32), axis=1).astype(jnp.float32)
    coarse_means = (coarse_sums + old_coarse.astype(jnp.float32)) / (coarse_totals + 1.0)[:, None]
    squares = lax.psum(jnp.sum(coarse_means * coarse_means, axis=1), "grp")
    total_width = quarter * lax.axis_size("grp")
    unit_part = (coarse_means * lax.rsqrt(squares / total_width + 1e-06)[:, None]).astype(
        jnp.bfloat16
    )
    coarse_dirs = lax.all_gather(unit_part, "grp", axis=1, tiled=True)
    return (new_fine, coarse_dirs)


def solution(mesh):
    in_specs = (
        P("rows", "grp"),
        P("rows"),
        P("rows", None),
        P("rows", "grp"),
        P("rows"),
        P("rows", "grp"),
    )
    out_specs = (P("rows", "grp"), P("rows", None))
    return jax.shard_map(
        on_device, mesh=mesh, in_specs=in_specs, out_specs=out_specs, check_vma=False
    )
```

```python
import functools
import math

import jax
import jax.numpy as jnp
from jax import lax
from jax.experimental import pallas as pl
from jax.experimental.pallas import tpu as pltpu
from jax.sharding import PartitionSpec as P

MESH = pl.DeviceIdType.MESH
LANES = 128


def neighbours(me):
    core, x, y = me % 2, (me // 2) % 2, me // 4
    other_x, other_y = 1 - x, 1 - y
    partner = 1 - core + 2 * x + 4 * y
    along = {
        (0, 0): me,
        (1, 0): core + 2 * other_x + 4 * y,
        (0, 1): core + 2 * x + 4 * other_y,
        (1, 1): core + 2 * other_x + 4 * other_y,
    }
    return partner, along


FIRST = ((1, 1, 0), (1, 1, 1), (1, 0, 0), (0, 1, 1), (1, 0, 1), (0, 1, 0))
AWAY = ((1, 1), (1, 0), (0, 1))
META = 8
FINE_DEPTH = 9
COARSE_DEPTH = 8


def one_hot(index, ids):
    low = jnp.clip(ids, -1, index.shape[0]).astype(jnp.int16)
    same = index == jnp.broadcast_to(low, index.shape)
    return jnp.where(same, jnp.ones((), jnp.bfloat16), jnp.zeros((), jnp.bfloat16))


def levels_kernel(
    tiles,
    emb,
    fine_local,
    sent,
    coarse_ids,
    old,
    old_coarse,
    out,
    dirs,
    other_emb,
    ids,
    other_ids,
    first_tile,
    other_first,
    acc,
    hits,
    away,
    landed,
    counts,
    own_counts,
    landed_counts,
    other_fine,
    coarse_away,
    coarse_landed,
    coarse_counts,
    coarse_counts_landed,
    means,
    squares,
    swap_send,
    swap_recv,
    meta_sem,
    send_sem,
    recv_sem,
    count_send,
    count_recv,
    fine_send,
    fine_recv,
    coarse_send,
    coarse_recv,
    coarse_count_send,
    coarse_count_recv,
    means_send,
    means_recv,
    squares_send,
    squares_recv,
):
    me = lax.axis_index("rows")
    slab = lax.axis_index("grp")
    slabs = lax.axis_size("grp")
    partner, along = neighbours(me)
    fine_dev, width = old.shape
    half = fine_dev // 2
    coarse_dev = old_coarse.shape[0]
    label_rows = emb.shape[0]
    fine_tiles = out.shape[0]
    others = [(slab + step) % slabs for step in range(1, slabs)]

    barrier = pltpu.get_barrier_semaphore()
    mates = [partner] + [along[quad] for quad in AWAY]
    for mate in mates:
        pl.semaphore_signal(barrier, inc=1, device_id={"rows": mate}, device_id_type=MESH)
    for other in others:
        pl.semaphore_signal(barrier, inc=1, device_id={"grp": other}, device_id_type=MESH)
    pl.semaphore_wait(barrier, len(mates) + len(others))

    def remote(src, dst, send, recv, target, axis="rows"):
        return pltpu.make_async_remote_copy(
            src_ref=src,
            dst_ref=dst,
            send_sem=send,
            recv_sem=recv,
            device_id={axis: target},
            device_id_type=MESH,
        )

    swaps = [
        remote(ids, other_ids, swap_send.at[0], swap_recv.at[0], partner),
        remote(emb, other_emb, swap_send.at[1], swap_recv.at[1], partner),
    ]
    swaps[1].start()
    place = lax.broadcasted_iota(jnp.int32, fine_local.shape, 0) * LANES
    place = place + lax.broadcasted_iota(jnp.int32, fine_local.shape, 2)
    lane = lax.broadcasted_iota(jnp.int32, (1, LANES), 1)
    owner = jnp.zeros_like(place)
    first = jnp.zeros_like(lane)
    end = 0
    for peer in range(sent.shape[1]):
        tile = jnp.minimum(end // LANES, label_rows - tiles)
        first_tile[peer] = tile
        first = jnp.where(lane == peer, tile, first)
        end = end + sent[0, peer]
        owner = owner + jnp.where(end <= place, 1, 0)
    ids[pl.ds(0, label_rows)] = owner * fine_dev + fine_local[...]
    ids[pl.ds(label_rows, META)] = jnp.zeros((META, 1, LANES), jnp.int32)
    ids[label_rows] = first
    ids[pl.ds(label_rows + META, fine_tiles)] = coarse_ids[...]
    swaps[0].start()
    counts[...] = jnp.zeros_like(counts)
    coarse_counts[...] = jnp.zeros_like(coarse_counts)
    index = lax.broadcasted_iota(jnp.int32, (half, LANES), 0).astype(jnp.int16)

    def add_tiles(total, hit, rows_of, ids_of, steps, depth, sides):
        @pl.loop(0, steps)
        def _(step):
            hots, rows = [], []
            for part in range(depth):
                for side in sides:
                    hots.append(one_hot(index, ids_of(side, step * depth + part)))
                    rows.append(rows_of(side, step * depth + part))
            hit[...] += functools.reduce(jnp.add, hots)
            total[...] += jnp.dot(
                jnp.concatenate(hots, axis=1),
                jnp.concatenate(rows, axis=0),
                preferred_element_type=jnp.float32,
            )

    def hit_row(hit):
        return lax.dot_general(
            jnp.ones((8, LANES), jnp.bfloat16),
            hit[...],
            (((1,), (1,)), ((), ())),
            preferred_element_type=jnp.float32,
        )[0:1]

    def add_rows(owner, part, total, hit, sides):
        base = owner * fine_dev + part * half

        def start_of(side):
            return first_tile[owner] if side == 0 else other_first[0, 0, owner]

        start = {side: start_of(side) for side in sides}

        def rows_of(side, tile):
            return (emb, other_emb)[side][start[side] + tile]

        def ids_of(side, tile):
            return (ids, other_ids)[side][start[side] + tile] - base

        if 0 in sides:
            total[...] = jnp.zeros_like(total)
            hit[...] = jnp.zeros_like(hit)
        add_tiles(total, hit, rows_of, ids_of, tiles // FINE_DEPTH, FINE_DEPTH, sides)

    for slot, (qx, qy, part) in enumerate(FIRST[:2]):
        add_rows(along[qx, qy], part, acc.at[slot], hits.at[slot], (0,))
    swaps[0].wait_recv()
    meta = pltpu.make_async_copy(other_ids.at[pl.ds(label_rows, META)], other_first, meta_sem)
    meta.start()
    meta.wait()
    swaps[1].wait_recv()

    sends = []
    for slot, (qx, qy, part) in enumerate(FIRST):
        at = slot if slot < 2 else 0
        sides = (1,) if slot < 2 else (0, 1)
        add_rows(along[qx, qy], part, acc.at[at], hits.at[at], sides)
        counts[pl.ds(slot, 1), :] = hit_row(hits.at[at])
        if slot == 5:
            count_copies = []
            for place, quad in enumerate(AWAY):
                copy = remote(
                    counts,
                    landed_counts.at[place],
                    count_send.at[place],
                    count_recv.at[place],
                    along[quad],
                )
                copy.start()
                count_copies.append(copy)
        if slot >= 4:
            sends[5 - slot].wait_recv()
            away[slot] = (acc[0] + landed[5 - slot].astype(jnp.float32)).astype(jnp.bfloat16)
        else:
            away[slot] = acc[at].astype(jnp.bfloat16)
        target = along[1, 0] if slot % 2 == 0 else along[0, 1]
        copy = remote(away.at[slot], landed.at[slot], send_sem.at[slot], recv_sem.at[slot], target)
        copy.start()
        sends.append(copy)
    for part in range(2):
        add_rows(me, part, acc.at[part], hits.at[0], (0, 1))
        own_counts[pl.ds(part, 1), :] = hit_row(hits.at[0])
    for copy in count_copies:
        copy.wait_recv()

    def column(row):
        return jnp.broadcast_to(row, (LANES, row.shape[1])).T

    fine_swaps = []
    for part in range(2):
        seen = own_counts[pl.ds(part, 1), :]
        for place, quad in enumerate(AWAY):
            row = FIRST.index(quad + (part,))
            seen = seen + landed_counts[place, pl.ds(row, 1), :]
        divisor = jnp.concatenate([column(seen + 1.0)] * (width // LANES), axis=1)
        near, far = (2, 5) if part == 0 else (3, 4)
        sends[near].wait_recv()
        sends[far].wait_recv()
        total = acc[part] + landed[near].astype(jnp.float32) + landed[far].astype(jnp.float32)
        total = total + old[pl.ds(part * half, half), :].astype(jnp.float32)
        span = pl.ds(part * (fine_tiles // 2), fine_tiles // 2)
        out[span] = (total / divisor).astype(jnp.bfloat16).reshape(-1, LANES, width)
        copy = remote(
            out.at[span], other_fine.at[span], fine_send.at[part], fine_recv.at[part], partner
        )
        copy.start()
        fine_swaps.append(copy)

    quads = AWAY + ((0, 0),)
    acc[0] = jnp.zeros_like(acc[0])
    hits[0] = jnp.zeros_like(hits[0])
    for copy in fine_swaps:
        copy.wait_recv()

    def place_of(coarse):
        owner = coarse // coarse_dev
        row = jnp.full_like(coarse, -1)
        for order, quad in enumerate(quads):
            inside = coarse - along[quad] * coarse_dev
            row = jnp.where(owner == along[quad], inside + order * coarse_dev, row)
        return row

    def fine_rows(side, tile):
        return (out, other_fine)[side][tile]

    def coarse_places(side, tile):
        return place_of((ids, other_ids)[side][label_rows + META + tile])

    steps = fine_tiles // COARSE_DEPTH
    add_tiles(acc.at[0], hits.at[0], fine_rows, coarse_places, steps, COARSE_DEPTH, (0, 1))
    coarse_counts[pl.ds(0, 1), :] = hit_row(hits.at[0])
    coarse_copies = []
    for order, quad in enumerate(AWAY):
        coarse_away[order] = acc[0, pl.ds(order * coarse_dev, coarse_dev), :].astype(jnp.bfloat16)
        for copy in (
            remote(
                coarse_counts,
                coarse_counts_landed.at[order],
                coarse_count_send.at[order],
                coarse_count_recv.at[order],
                along[quad],
            ),
            remote(
                coarse_away.at[order],
                coarse_landed.at[order],
                coarse_send.at[order],
                coarse_recv.at[order],
                along[quad],
            ),
        ):
            copy.start()
            coarse_copies.append(copy)
    total = acc[0, pl.ds(3 * coarse_dev, coarse_dev), :] + old_coarse[...].astype(jnp.float32)
    seen = coarse_counts[pl.ds(0, 1), pl.ds(3 * coarse_dev, coarse_dev)]
    for copy in coarse_copies:
        copy.wait_recv()
    for order in range(3):
        total = total + coarse_landed[order].astype(jnp.float32)
        seen = seen + coarse_counts_landed[order, pl.ds(0, 1), pl.ds(order * coarse_dev, coarse_dev)]
    mean = total / jnp.concatenate([column(seen + 1.0)] * (width // LANES), axis=1)
    means[slab] = mean.astype(jnp.bfloat16)
    square = jnp.sum(mean * mean, axis=1, keepdims=True)
    squares[slab] = jnp.broadcast_to(square, (coarse_dev, LANES)).T[0:8]
    mean_copies = []
    for order, other in enumerate(others):
        for copy in (
            remote(
                squares.at[slab],
                squares.at[slab],
                squares_send.at[order],
                squares_recv.at[order],
                other,
                "grp",
            ),
            remote(
                means.at[slab],
                means.at[slab],
                means_send.at[order],
                means_recv.at[order],
                other,
                "grp",
            ),
        ):
            copy.start()
            mean_copies.append(copy)
    for copy in mean_copies:
        copy.wait_recv()
    square = squares[0, 0:1]
    for at in range(1, slabs):
        square = square + squares[at, 0:1]
    scale = column(lax.rsqrt(square / (width * slabs) + 1e-06))
    scale = jnp.concatenate([scale] * (width // LANES), axis=1)
    for at in range(slabs):
        dirs[:, at * width : (at + 1) * width] = (means[at].astype(jnp.float32) * scale).astype(
            jnp.bfloat16
        )
    for copy in swaps + sends + count_copies + fine_swaps + coarse_copies + mean_copies:
        copy.wait_send()


def tree_levels(embeddings, fine_local, send_counts, old_fine, coarse_ids, old_coarse):
    peers = lax.axis_size("rows")
    slabs = lax.axis_size("grp")
    per_dev, width = embeddings.shape
    fine_dev = old_fine.shape[0]
    coarse_dev = old_coarse.shape[0]
    half = fine_dev // 2
    capacity = 2 * per_dev // peers
    tiles = -(-(capacity // LANES + 1) // FINE_DEPTH) * FINE_DEPTH
    label_rows = per_dev // LANES
    fine_tiles = fine_dev // LANES
    id_shape = (label_rows + META + fine_tiles, 1, LANES)
    tiled = embeddings.reshape(label_rows, LANES, width)
    vmem = pl.BlockSpec(memory_space=pltpu.VMEM)
    dma = pltpu.SemaphoreType.DMA
    f32, bf16 = jnp.float32, jnp.bfloat16
    new_fine, dirs = pl.pallas_call(
        functools.partial(levels_kernel, tiles),
        out_shape=[
            jax.ShapeDtypeStruct((fine_tiles, LANES, width), bf16),
            jax.ShapeDtypeStruct((coarse_dev, slabs * width), bf16),
        ],
        in_specs=[vmem, vmem, pl.BlockSpec(memory_space=pltpu.SMEM), vmem, vmem, vmem],
        out_specs=[vmem, vmem],
        scratch_shapes=[
            pltpu.VMEM(tiled.shape, bf16),
            pltpu.VMEM(id_shape, jnp.int32),
            pltpu.VMEM(id_shape, jnp.int32),
            pltpu.SMEM((peers,), jnp.int32),
            pltpu.SMEM((META, 1, LANES), jnp.int32),
            pltpu.VMEM((2, half, width), f32),
            pltpu.VMEM((2, half, LANES), bf16),
            pltpu.VMEM((6, half, width), bf16),
            pltpu.VMEM((6, half, width), bf16),
            pltpu.VMEM((8, half), f32),
            pltpu.VMEM((8, half), f32),
            pltpu.VMEM((3, 8, half), f32),
            pltpu.VMEM((fine_tiles, LANES, width), bf16),
            pltpu.VMEM((3, coarse_dev, width), bf16),
            pltpu.VMEM((3, coarse_dev, width), bf16),
            pltpu.VMEM((8, half), f32),
            pltpu.VMEM((3, 8, half), f32),
            pltpu.VMEM((slabs, coarse_dev, width), bf16),
            pltpu.VMEM((slabs, 8, coarse_dev), f32),
            dma((2,)),
            dma((2,)),
            dma,
            dma((6,)),
            dma((6,)),
            dma((3,)),
            dma((3,)),
            dma((2,)),
            dma((2,)),
            dma((3,)),
            dma((3,)),
            dma((3,)),
            dma((3,)),
            dma((slabs - 1,)),
            dma((slabs - 1,)),
            dma((slabs - 1,)),
            dma((slabs - 1,)),
        ],
        compiler_params=pltpu.CompilerParams(
            collective_id=0, has_side_effects=True, vmem_limit_bytes=48 * 1024 * 1024
        ),
    )(
        tiled,
        fine_local.reshape(label_rows, 1, LANES),
        send_counts,
        coarse_ids.reshape(fine_tiles, 1, LANES),
        old_fine,
        old_coarse,
    )
    return new_fine.reshape(old_fine.shape), dirs


def onehot_sums(arrived, arrived_labels, fine_dev):
    slot_total = arrived.shape[0]
    width = arrived.shape[1]
    block_rows = math.gcd(slot_total, 2048)
    block_count = slot_total // block_rows
    cluster_index = jnp.arange(fine_dev, dtype=jnp.int32)

    def accumulate(state_pair, pieces):
        fine_sums, totals = state_pair
        row_block, label_block = pieces
        onehot = cluster_index[:, None] == label_block[None, :]
        fine_sums = fine_sums + jnp.dot(
            onehot.astype(jnp.bfloat16), row_block, preferred_element_type=jnp.float32
        )
        totals = totals + jnp.sum(onehot.astype(jnp.int32), axis=1)
        return ((fine_sums, totals), None)

    start_state = (jnp.zeros((fine_dev, width), jnp.float32), jnp.zeros((fine_dev,), jnp.int32))
    (fine_sums, totals), _ = lax.scan(
        accumulate,
        start_state,
        (
            arrived.reshape(block_count, block_rows, width),
            arrived_labels.reshape(block_count, block_rows),
        ),
    )
    return (fine_sums, totals.astype(jnp.float32))


def exchanged_rows(embeddings, fine_local, send_counts, old_fine):
    peer_count = lax.axis_size("rows")
    per_dev = embeddings.shape[0]
    quarter = embeddings.shape[1]
    fine_dev = old_fine.shape[0]
    capacity = 2 * per_dev // peer_count
    counts = send_counts[0]
    starts = jnp.cumsum(counts) - counts
    offset = jnp.arange(capacity, dtype=jnp.int32)
    is_live = offset[None, :] < counts[:, None]
    padded_rows = jnp.concatenate(
        [embeddings, jnp.zeros((capacity, quarter), jnp.bfloat16)], axis=0
    )
    padded_local = jnp.concatenate([fine_local, jnp.zeros((capacity,), jnp.int32)], axis=0)

    def take_segment(first_row):
        segment_rows = lax.dynamic_slice_in_dim(padded_rows, first_row, capacity, 0)
        segment_labels = lax.dynamic_slice_in_dim(padded_local, first_row, capacity, 0)
        return (segment_rows, segment_labels)

    outgoing, raw_labels = lax.map(take_segment, starts)
    outgoing = jnp.where(is_live[:, :, None], outgoing, jnp.zeros((), jnp.bfloat16))
    labels = jnp.where(is_live, raw_labels, -1)
    arrived, arrived_labels = (
        lax.all_to_all(outgoing, "rows", split_axis=0, concat_axis=0, tiled=True),
        lax.all_to_all(labels, "rows", split_axis=0, concat_axis=0, tiled=True),
    )
    fine_sums, totals = onehot_sums(
        arrived.reshape(-1, quarter), arrived_labels.reshape(-1), fine_dev
    )
    new_fine = ((fine_sums + old_fine.astype(jnp.float32)) / (totals + 1.0)[:, None]).astype(
        jnp.bfloat16
    )
    return new_fine


def on_device(embeddings, fine_local, send_counts, old_fine, coarse_ids, old_coarse):
    peer_count = lax.axis_size("rows")
    quarter = embeddings.shape[1]
    fine_dev = old_fine.shape[0]
    coarse_dev = old_coarse.shape[0]
    dense = 2 * embeddings.shape[0] // peer_count >= fine_dev
    if peer_count == 8 and dense and 8 * coarse_dev == fine_dev:
        return tree_levels(embeddings, fine_local, send_counts, old_fine, coarse_ids, old_coarse)
    new_fine = exchanged_rows(embeddings, fine_local, send_counts, old_fine)
    owners = coarse_ids // coarse_dev
    local_id = coarse_ids - owners * coarse_dev
    capacity_two = 2 * fine_dev // peer_count
    member = (owners[:, None] == jnp.arange(peer_count, dtype=jnp.int32)[None, :]).astype(jnp.int32)
    slot_rank = jnp.sum(jnp.cumsum(member, axis=0) * member, axis=1) - 1
    slot_pos = owners * capacity_two + slot_rank
    placement = (
        jnp.arange(peer_count * capacity_two, dtype=jnp.int32)[:, None] == slot_pos[None, :]
    ).astype(jnp.bfloat16)
    outgoing_two = jnp.dot(placement, new_fine, preferred_element_type=jnp.float32).astype(
        jnp.bfloat16
    )
    label_plus = jnp.dot(
        placement, (local_id + 1).astype(jnp.bfloat16), preferred_element_type=jnp.float32
    )
    labels_two = label_plus.astype(jnp.int32) - 1
    received, received_labels = (
        lax.all_to_all(
            outgoing_two.reshape(peer_count, capacity_two, quarter),
            "rows",
            split_axis=0,
            concat_axis=0,
            tiled=True,
        ),
        lax.all_to_all(
            labels_two.reshape(peer_count, capacity_two),
            "rows",
            split_axis=0,
            concat_axis=0,
            tiled=True,
        ),
    )
    onehot_two = (
        jnp.arange(coarse_dev, dtype=jnp.int32)[:, None] == received_labels.reshape(-1)[None, :]
    )
    coarse_sums = jnp.dot(
        onehot_two.astype(jnp.bfloat16),
        received.reshape(-1, quarter),
        preferred_element_type=jnp.float32,
    )
    coarse_totals = jnp.sum(onehot_two.astype(jnp.int32), axis=1).astype(jnp.float32)
    coarse_means = (coarse_sums + old_coarse.astype(jnp.float32)) / (coarse_totals + 1.0)[:, None]
    squares = lax.psum(jnp.sum(coarse_means * coarse_means, axis=1), "grp")
    total_width = quarter * lax.axis_size("grp")
    unit_part = (coarse_means * lax.rsqrt(squares / total_width + 1e-06)[:, None]).astype(
        jnp.bfloat16
    )
    coarse_dirs = lax.all_gather(unit_part, "grp", axis=1, tiled=True)
    return (new_fine, coarse_dirs)


def solution(mesh):
    in_specs = (
        P("rows", "grp"),
        P("rows"),
        P("rows", None),
        P("rows", "grp"),
        P("rows"),
        P("rows", "grp"),
    )
    out_specs = (P("rows", "grp"), P("rows", None))
    return jax.shard_map(
        on_device, mesh=mesh, in_specs=in_specs, out_specs=out_specs, check_vma=False
    )
```
